32 devices in a mesh: tok: 8 (over z, y), head: 4 (over x, core).
Axes of the slice: x: 2, y: 2, z: 4, core: 2. Of those that a mesh axis runs over, the one named last changes fastest.
Arguments:
- hidden_in: bfloat16 [4096, 2048], P(('tok', 'head')), may hold values from -6 to 6
- context_len: int32 [8], P('tok'), may hold values from 1 to 2048, 8192 in all
- page_table: int32 [8, 16], P('tok'), may hold values from 0 to 15, as said below
- paged_cache: bfloat16 [2, 128, 128, 2048], P(None, 'tok', None, 'head'), may hold values from -139 to 139
- attn_gain: bfloat16 [2048], replicated, may hold values from 0.5 to 1.5
- proj_weight: bfloat16 [3, 2048, 2048], P(None, None, 'head'), may hold values from -0.125 to 0.125
- proj_bias: bfloat16 [3, 2048], P(None, 'head'), may hold values from -3 to 3
- out_weight: bfloat16 [2048, 2048], P('head'), may hold values from -0.125 to 0.125
- mlp_gain: bfloat16 [2048], replicated, may hold values from 0.5 to 1.5
- expert_ids: int32 [4096, 4], P(('tok', 'head')), may hold values from 0 to 15, all different within a row; in each aligned block of 128 rows (0 to 127, 128 to 255, ...) at most 40 rows name the same one
- route_weight: float32 [4096, 4], P(('tok', 'head')), may hold values from 0.05 to 0.5
- w_experts_in: bfloat16 [32, 2048, 1408], P(('tok', 'head')), may hold values from -0.125 to 0.125
- w_experts_out: bfloat16 [32, 704, 2048], P(('tok', 'head')), may hold values from -0.15625 to 0.15625
- w_shared_in: bfloat16 [2048, 2, 5632], P(None, None, 'head'), may hold values from -0.125 to 0.125
- w_shared_out: bfloat16 [5632, 2048], P('head'), may hold values from -0.078125 to 0.078125
- shared_gate: bfloat16 [2048], replicated, may hold values from -0.125 to 0.125
Outputs:
- layer_out: bfloat16 [4096, 2048], P(('tok', 'head'))
The draws below stay inside these ranges and needn't reach their ends.
Inputs may be any that keep to these rules, and one draw needn't show every extreme that they name: `page_table`: each row is a permutation of the pool's pages. `context_len`: some request has exactly 2048 cached tokens. `expert_ids`: the experts of a row differ; within the 128 rows of one device no expert is named more than 40 times, a bound that some block reaches.
All inputs are finite; a program needn't handle non-finite values. No bound on the sum of `context_len` on one device may be relied on, other than what follows from the above.
Results may differ from the reference program's by a relative error of at most 0.02.
Values may be sent and summed in bfloat16 or wider, within the bound.
A program may use at most 128 MiB of HBM per device.

```python
import math
import jax
import jax.numpy as jnp
import numpy as np
from jax import lax

D = 2048
HEADS = 16
HD = 128
MOE_FF = 1408
SHARED_FF = 5632
TOP = 4
TOK_DEV = 128
CTX = 2048
PAGE = 128
EXPERTS = 16
HALF = 704
CAP = 40
REQS = 8
STRETCH = 512
TOKENS = 4096
PAGES_DEV = 16
N_TOK = 8
N_HEAD = 4


def draw_page_table(key, part):
    subkeys = jax.random.split(key, REQS)

    def single_row(subkey):
        return jax.random.permutation(subkey, PAGES_DEV)
    return jax.vmap(single_row)(subkeys).astype(jnp.int32)


def draw_paged_cache(key, part):
    shape = (2, REQS * PAGES_DEV, PAGE, HEADS * HD)
    base = jnp.clip(jax.random.normal(key, shape, jnp.float32), -6.0, 6.0)
    return base.astype(jnp.bfloat16)


def shard_levels(key, dims, cuts, smallest, top_value):
    level, own = 1.0, jax.random.fold_in(key, 6)
    for dim, parts in cuts:
        steps = jnp.exp(jax.random.uniform(jax.random.fold_in(own, dim), (parts,), jnp.float32, smallest / len(cuts), top_value / len(cuts)))
        level = level * jnp.repeat(steps, dims[dim] // parts).reshape([-1 if axis == dim else 1 for axis in range(len(dims))])
    return level


def split_up(amount, total, bound, lean):
    loads = [(1 << 20) // math.isqrt(rank ** lean) + 1 for rank in range(2, amount + 1)]
    spare, given = total - bound - (amount - 1), [1] * (amount - 1)
    while spare > 0:
        candidates = [i for i in range(amount - 1) if given[i] < bound]
        whole, remaining = sum([loads[i] for i in candidates]), spare
        for i in candidates:
            addition = min(bound - given[i], max(1, remaining * loads[i] // whole), spare)
            given[i] = given[i] + addition
            spare = spare - addition
    return np.array([bound] + given)


def ragged(key, count, total, reach, skew):
    if count == 2:
        one = jax.random.randint(key, (), max(1, total - reach), min(reach, total - 1) + 1)
        return jnp.stack([one, total - one])
    sizes = jnp.asarray(split_up(count, total, reach, skew), jnp.int32)
    twos = (count - 1) // 2
    source_of, sink = sizes[1:1 + 2 * twos:2], sizes[2:2 + 2 * twos:2]
    margin = jnp.minimum(source_of - 1, reach - sink)
    passed = jax.random.randint(jax.random.fold_in(key, 1), (twos,), 0, 1 << 20) % (margin + 1)
    sizes = sizes.at[1:1 + 2 * twos:2].set(source_of - passed).at[2:2 + 2 * twos:2].set(sink + passed)
    return sizes[jax.random.permutation(jax.random.fold_in(key, 2), count)]


def deal_out(stream_key, own, number, rows, amount, top, most, lean):
    sequence = jax.random.permutation(stream_key, amount)
    crowded, common = portions_of(amount, rows * top, most, lean, True), portions_of(amount, rows * top, most, lean, False)
    places = jnp.arange(amount)

    def named(sizes, offset_by):
        used = int((sizes > 0).sum())
        fixed = max(1, used // 4)
        shifted = fixed + (places - fixed + offset_by * (used - fixed)) % max(1, amount - fixed)
        return jnp.zeros((amount,), jnp.int32).at[sequence[jnp.where(places < fixed, places, shifted)]].set(jnp.asarray(sizes, jnp.int32))

    sizes = jnp.where(number % 4 == 0, named(crowded, number // 4), named(common, number - number // 4 - 1))
    mixed = jax.random.permutation(jax.random.fold_in(own, 3), amount)
    donor, sink = mixed[0:amount // 2 * 2:2], mixed[1:amount // 2 * 2:2]
    room = jnp.minimum(sizes[donor] - 1, most - sizes[sink]) // 2
    room = jnp.where((donor == sequence[0]) | (sink == sequence[0]) | (sizes[sink] == 0), 0, jnp.maximum(room, 0))
    shifted = jax.random.randint(jax.random.fold_in(own, 4), (amount // 2,), 0, 1 << 20) % (room + 1)
    sizes = sizes.at[donor].add(-shifted).at[sink].add(shifted)
    items = jnp.searchsorted(jnp.cumsum(sizes), jnp.arange(rows * top), side="right").astype(jnp.int32)
    listing = items.reshape(top, rows).T
    listing = listing[jax.random.permutation(jax.random.fold_in(own, 1), rows)]
    offset_by = jax.random.randint(jax.random.fold_in(own, 2), (rows, 1), 0, top)
    return jnp.take_along_axis(listing, (jnp.arange(top)[None, :] + offset_by) % top, axis=1)


def portions_of(count, total, most, slope, full):
    portions = [(1 << 20) // math.isqrt(standing ** slope) + 1 for standing in range(1, count + 1)]
    largest = most if full else min(most, max(-(-total // count), total * portions[0] // sum(portions)))
    least = 1 if total - largest >= count - 1 else 0
    given, surplus = [largest] + [least] * (count - 1), total - largest - least * (count - 1)
    while surplus > 0:
        movable = [i for i in range(1, count) if given[i] < largest] or [i for i in range(1, count) if given[i] < most]
        whole, left = sum([portions[i] for i in movable]), surplus
        for i in movable:
            extra = min(most - given[i], max(1, left * portions[i] // whole), surplus)
            given[i] = given[i] + extra
            surplus = surplus - extra
    return np.array(given)


def gaussian(own_key, shape, scale, bound, cuts=(), kind=jnp.bfloat16):
    values = scale * jax.random.normal(own_key, shape, jnp.float32)
    if cuts:
        values = values * shard_levels(own_key, shape, cuts, -0.22, 0.18)
    return jnp.clip(values, -bound, bound).astype(kind)


def setup_inputs(seed: int = 0) -> dict:
    splits = jax.random.split(jax.random.key(seed), 17)
    hidden_in = gaussian(splits[0], (TOKENS, D), 1.0, 6.0, ((0, 32),))
    context_len = ragged(splits[1], REQS, REQS * CTX // 2, CTX, 1).astype(jnp.int32)
    page_table = draw_page_table(jax.random.fold_in(splits[16], 71), 0)
    paged_cache = draw_paged_cache(jax.random.fold_in(splits[16], 71), 0)
    attn_gain = jnp.clip(1.0 + 0.1 * jax.random.normal(splits[4], (D,), jnp.float32), 0.5, 1.5).astype(jnp.bfloat16)
    proj_weight = gaussian(splits[5], (3, D, HEADS * HD), D ** -0.5, 0.125, ((2, 4),))
    proj_bias = gaussian(splits[6], (3, HEADS * HD), 0.5, 3.0, ((1, 4),))
    out_weight = gaussian(splits[7], (HEADS * HD, D), (HEADS * HD) ** -0.5, 0.125, ((0, 4),))
    mlp_gain = jnp.clip(1.0 + 0.1 * jax.random.normal(splits[8], (D,), jnp.float32), 0.5, 1.5).astype(jnp.bfloat16)
    expert_ids_keys = jax.random.split(jax.random.fold_in(splits[9], 1), TOKENS // TOK_DEV)
    expert_ids_turns = jax.random.permutation(jax.random.fold_in(splits[9], 3), TOKENS // TOK_DEV)
    expert_ids = jax.vmap(lambda own, number: deal_out(jax.random.fold_in(splits[9], 2), own, number, TOK_DEV, EXPERTS, TOP, CAP, 2))(expert_ids_keys, expert_ids_turns).reshape((TOKENS, TOP))
    route_weight = jnp.clip(0.05 + 0.45 * jax.random.uniform(splits[10], (TOKENS, TOP), jnp.float32) ** shard_levels(splits[10], (TOKENS, TOP), ((0, 32),), -0.2, 0.2), 0.05, 0.5)
    w_experts_in = gaussian(splits[11], (EXPERTS * 2, D, MOE_FF), D ** -0.5, 0.125, ((0, 32),))
    w_experts_out = gaussian(splits[12], (EXPERTS * 2, HALF, D), MOE_FF ** -0.5, 0.15625, ((0, 32),))
    w_shared_in = gaussian(splits[13], (D, 2, SHARED_FF), D ** -0.5, 0.125, ((2, 4),))
    w_shared_out = gaussian(splits[14], (SHARED_FF, D), SHARED_FF ** -0.5, 0.078125, ((0, 4),))
    shared_gate = gaussian(splits[15], (D,), D ** -0.5, 0.125)
    return {"hidden_in": hidden_in, "context_len": context_len, "page_table": page_table, "paged_cache": paged_cache, "attn_gain": attn_gain, "proj_weight": proj_weight, "proj_bias": proj_bias, "out_weight": out_weight, "mlp_gain": mlp_gain, "expert_ids": expert_ids, "route_weight": route_weight, "w_experts_in": w_experts_in, "w_experts_out": w_experts_out, "w_shared_in": w_shared_in, "w_shared_out": w_shared_out, "shared_gate": shared_gate}


EPS = 1e-06
THETA = 1000000.0

def rms_scale(values, gain):
    wide = values.astype(jnp.float32)
    spread = lax.optimization_barrier(jnp.mean(wide * wide, axis=-1, keepdims=True))
    return (wide * lax.rsqrt(spread + EPS) * gain.astype(jnp.float32)).astype(jnp.bfloat16)

def rotate(vectors, positions):
    middle = vectors.shape[-1] // 2
    frequency = THETA ** (-(jnp.arange(middle, dtype=jnp.float32) * 2.0 / vectors.shape[-1]))
    angles = positions.astype(jnp.float32)[:, None] * frequency[None, :]
    angles = jnp.concatenate([angles, angles], axis=-1)[:, None, :]
    turned = jnp.concatenate([-vectors[..., middle:], vectors[..., :middle]], axis=-1)
    return vectors * jnp.cos(angles) + turned * jnp.sin(angles)

def attend(queries, keys_all, values_all, context, span_len):
    row_count = queries.shape[0]
    head_count = queries.shape[1]
    head_size = queries.shape[2]
    block_rows = math.gcd(row_count, 512)
    block_count = row_count // block_rows
    scale = 1.0 / math.sqrt(head_size)
    key_pos = jnp.arange(keys_all.shape[0], dtype=jnp.int32)
    keys_wide = keys_all.astype(jnp.float32)
    values_wide = values_all.astype(jnp.float32)

    def one_block(items):
        query_block, start = items
        scores = jnp.einsum('qhd,khd->hqk', query_block.astype(jnp.float32), keys_wide) * scale
        query_pos = start + jnp.arange(block_rows, dtype=jnp.int32)
        allowed = jnp.where(key_pos[None, :] < span_len, key_pos[None, :] < context, key_pos[None, :] - span_len <= query_pos[:, None])
        scores = jnp.where(allowed[None], scores, -1e+30)
        largest = lax.optimization_barrier(jnp.max(scores, axis=-1, keepdims=True))
        weights = jnp.where(allowed[None], jnp.exp(scores - largest), 0.0)
        probs = (weights / lax.optimization_barrier(jnp.sum(weights, axis=-1, keepdims=True))).astype(jnp.bfloat16)
        return jnp.einsum('hqk,khd->qhd', probs.astype(jnp.float32), values_wide).astype(jnp.bfloat16)
    starts = jnp.arange(block_count, dtype=jnp.int32) * block_rows
    result = lax.map(one_block, (queries.reshape(block_count, block_rows, head_count, head_size), starts))
    return result.reshape(row_count, head_count, head_size)

def reference(hidden_in, context_len, page_table, paged_cache, attn_gain, proj_weight, proj_bias, out_weight, mlp_gain, expert_ids, route_weight, w_experts_in, w_experts_out, w_shared_in, w_shared_out, shared_gate):
    normed = rms_scale(hidden_in, attn_gain)
    positions = jnp.repeat(context_len, STRETCH) + jnp.tile(jnp.arange(STRETCH, dtype=jnp.int32), REQS)
    projected = jnp.einsum('td,cdf->ctf', normed.astype(jnp.float32), proj_weight.astype(jnp.float32)) + proj_bias.astype(jnp.float32)[:, None, :]
    queries = rotate(projected[0].reshape(TOKENS, HEADS, HD), positions).astype(jnp.bfloat16)
    new_keys = rotate(projected[1].reshape(TOKENS, HEADS, HD), positions).astype(jnp.bfloat16)
    new_values = projected[2].reshape(TOKENS, HEADS, HD).astype(jnp.bfloat16)
    pools = jnp.moveaxis(paged_cache.reshape(2, REQS, PAGES_DEV, PAGE, HEADS * HD), 1, 0)

    def per_request(items):
        query_rows, key_rows, value_rows, pool, table, context = items
        ordered = jnp.take(pool, table, axis=1).reshape(2, CTX, HEADS, HD)
        keys_all = jnp.concatenate([ordered[0], key_rows], axis=0)
        values_all = jnp.concatenate([ordered[1], value_rows], axis=0)
        return attend(query_rows, keys_all, values_all, context, CTX)
    heads_out = lax.map(per_request, (queries.reshape(REQS, STRETCH, HEADS, HD), new_keys.reshape(REQS, STRETCH, HEADS, HD), new_values.reshape(REQS, STRETCH, HEADS, HD), pools, page_table, context_len))
    group_width = HEADS // N_HEAD * HD
    heads_grouped = jnp.moveaxis(heads_out.reshape(TOKENS, N_HEAD, group_width), 1, 0)
    out_weights = out_weight.reshape(N_HEAD, group_width, D)

    def attn_group(total, pieces):
        rows_group, weight_group = pieces
        partial_value = jnp.dot(rows_group, weight_group, preferred_element_type=jnp.float32).astype(jnp.bfloat16)
        return (total + lax.optimization_barrier(partial_value).astype(jnp.float32), None)
    attn_sum = lax.scan(attn_group, jnp.zeros((TOKENS, D), jnp.float32), (heads_grouped, out_weights))[0]
    resid = (hidden_in.astype(jnp.float32) + attn_sum).astype(jnp.bfloat16)
    mixed = rms_scale(resid, mlp_gain)
    shared_width = SHARED_FF // N_HEAD
    shared_in = jnp.transpose(w_shared_in.reshape(D, 2, N_HEAD, shared_width), (2, 0, 1, 3))
    shared_out = w_shared_out.reshape(N_HEAD, shared_width, D)
    mixed_wide = mixed.astype(jnp.float32)

    def shared_group(total, pieces):
        weight_in, weight_out = pieces
        inner = jnp.einsum('td,dcf->tcf', mixed_wide, weight_in.astype(jnp.float32))
        activated = (jax.nn.silu(inner[:, 0]) * inner[:, 1]).astype(jnp.bfloat16)
        partial_value = jnp.dot(activated, weight_out, preferred_element_type=jnp.float32).astype(jnp.bfloat16)
        return (total + lax.optimization_barrier(partial_value).astype(jnp.float32), None)
    shared = lax.scan(shared_group, jnp.zeros((TOKENS, D), jnp.float32), (shared_in, shared_out))[0]
    gate = jax.nn.sigmoid(jnp.dot(mixed, shared_gate, preferred_element_type=jnp.float32))
    copies = TOKENS * TOP
    limit = N_TOK * N_HEAD * CAP
    flat_ids = expert_ids.reshape(-1)
    padded = jnp.concatenate([mixed, jnp.zeros((1, D), jnp.bfloat16)], axis=0)
    weight_pad = jnp.concatenate([route_weight.reshape(-1), jnp.zeros((1,), jnp.float32)])

    def per_expert(total, expert):
        chosen = jnp.nonzero(flat_ids == expert, size=limit, fill_value=copies)[0].astype(jnp.int32)
        token_index = chosen // TOP
        picked = padded[token_index]
        weights = weight_pad[chosen]
        result = jnp.zeros((limit, D), jnp.float32)
        for half_index in range(2):
            weight_row = 2 * expert + half_index
            inner = jnp.dot(picked, w_experts_in[weight_row], preferred_element_type=jnp.float32)
            activated = (jax.nn.silu(inner[:, :HALF]) * inner[:, HALF:]).astype(jnp.bfloat16)
            partial_value = jnp.dot(activated, w_experts_out[weight_row], preferred_element_type=jnp.float32).astype(jnp.bfloat16)
            result = result + lax.optimization_barrier(partial_value).astype(jnp.float32)
        merged = lax.optimization_barrier(result.astype(jnp.bfloat16)).astype(jnp.float32)
        return (total.at[token_index].add(weights[:, None] * merged), None)
    routed = lax.scan(per_expert, jnp.zeros((TOKENS + 1, D), jnp.float32), jnp.arange(EXPERTS, dtype=jnp.int32))[0][:TOKENS]
    return (resid.astype(jnp.float32) + gate[:, None] * shared + routed).astype(jnp.bfloat16)
```

```python
import math

import jax
import jax.numpy as jnp
from jax import lax
from jax.experimental import pallas as pl
from jax.experimental.pallas import tpu as pltpu
from jax.sharding import PartitionSpec as P

HD = 128
BLOCK = 256
DEEP = (((1,), (1,)), ((), ()))
DOWN = (((0,), (0,)), ((), ()))


EPS = 1e-06
THETA = 1000000.0


def rms_scale(values, gain):
    wide = values.astype(jnp.float32)
    spread = jnp.mean(wide * wide, axis=-1, keepdims=True)
    return (wide * lax.rsqrt(spread + EPS) * gain.astype(jnp.float32)).astype(jnp.bfloat16)


def attend_kernel(
    table, context_len, rows, gain, weight, bias, cosines, sines, cache, out_weight, out, q_all, k_all, v_all
):
    stretch, width = rows.shape
    lanes = weight.shape[2]
    heads = lanes // HD
    pages, page = cache.shape[1], cache.shape[2]
    span = pages * page
    context = context_len[0]

    @pl.loop(0, pages)
    def _(index):
        place = table[0, index]
        at = pl.ds(pl.multiple_of(index * page, page), page)
        k_all[at, :] = cache[0, place]
        v_all[at, :] = cache[1, place]

    @pl.loop(0, stretch // BLOCK)
    def _(block):
        start = pl.multiple_of(block * BLOCK, BLOCK)
        at = pl.ds(start, BLOCK)
        new_at = pl.ds(pl.multiple_of(span + start, BLOCK), BLOCK)
        wide = rows[at, :].astype(jnp.float32)
        spread = jnp.mean(wide * wide, axis=-1, keepdims=True)
        normed = (wide * lax.rsqrt(spread + EPS) * gain[...]).astype(jnp.bfloat16)
        cos, sin = cosines[at, :], sines[at, :]
        for part, kept, place in ((0, q_all, at), (1, k_all, new_at), (2, v_all, new_at)):
            value = jnp.dot(normed, weight[part], preferred_element_type=jnp.float32) + bias[part]
            if part < 2:
                turned = []
                for head in range(heads):
                    one = value[:, head * HD : (head + 1) * HD]
                    turned.append(one * cos + pltpu.roll(one, HD // 2, 1) * sin)
                value = jnp.concatenate(turned, axis=1)
            kept[place, :] = value.astype(jnp.bfloat16)

    factor = math.log2(math.e) / math.sqrt(HD)

    @pl.loop(0, stretch // BLOCK)
    def _(block):
        start = pl.multiple_of(block * BLOCK, BLOCK)
        at = pl.ds(start, BLOCK)
        old_ok = lax.broadcasted_iota(jnp.int32, (BLOCK, span), 1) < context
        new_ok = lax.broadcasted_iota(jnp.int32, (BLOCK, stretch), 1) <= (
            lax.broadcasted_iota(jnp.int32, (BLOCK, stretch), 0) + start
        )
        found = []
        for head in range(heads):
            cols = slice(head * HD, (head + 1) * HD)
            query = q_all[at, cols]
            old = lax.dot_general(query, k_all[:span, cols], DEEP, preferred_element_type=jnp.float32)
            new = lax.dot_general(query, k_all[span:, cols], DEEP, preferred_element_type=jnp.float32)
            old = jnp.where(old_ok, old, -1e30)
            new = jnp.where(new_ok, new, -1e30)
            largest = jnp.maximum(
                jnp.max(old, axis=-1, keepdims=True), jnp.max(new, axis=-1, keepdims=True)
            )
            old = jnp.exp2((old - largest) * factor)
            new = jnp.exp2((new - largest) * factor)
            total = jnp.sum(old, axis=-1, keepdims=True) + jnp.sum(new, axis=-1, keepdims=True)
            value = jnp.dot(
                old.astype(jnp.bfloat16), v_all[:span, cols], preferred_element_type=jnp.float32
            ) + jnp.dot(
                new.astype(jnp.bfloat16), v_all[span:, cols], preferred_element_type=jnp.float32
            )
            found.append((value / total).astype(jnp.bfloat16))
        out[at, :] = jnp.dot(
            jnp.concatenate(found, axis=1), out_weight[...], preferred_element_type=jnp.float32
        ).astype(jnp.bfloat16)


def attend(gathered, context_len, page_table, cache, gain, weight, bias, out_weight):
    stretch, width = gathered.shape
    lanes = weight.shape[2]
    span = cache.shape[1] * cache.shape[2]
    frequency = THETA ** (-(jnp.arange(HD // 2, dtype=jnp.float32) * 2.0 / HD))
    positions = context_len[0] + jnp.arange(stretch, dtype=jnp.int32)
    angles = positions.astype(jnp.float32)[:, None] * frequency[None, :]
    cosines = jnp.tile(jnp.cos(angles), (1, 2))
    sines = jnp.sin(angles)
    sines = jnp.concatenate([-sines, sines], axis=1)
    smem = pl.BlockSpec(memory_space=pltpu.SMEM)
    vmem = pl.BlockSpec(memory_space=pltpu.VMEM)
    return pl.pallas_call(
        attend_kernel,
        out_shape=jax.ShapeDtypeStruct((stretch, width), jnp.bfloat16),
        in_specs=[smem, smem] + [vmem] * 8,
        out_specs=vmem,
        scratch_shapes=[
            pltpu.VMEM((stretch, lanes), jnp.bfloat16),
            pltpu.VMEM((span + stretch, lanes), jnp.bfloat16),
            pltpu.VMEM((span + stretch, lanes), jnp.bfloat16),
        ],
        compiler_params=pltpu.CompilerParams(vmem_limit_bytes=52 * 1024 * 1024),
        cost_estimate=pl.CostEstimate(
            flops=12 * 10**9, bytes_accessed=20 * 10**6, transcendentals=5 * 10**6
        ),
    )(
        page_table,
        context_len,
        gathered,
        gain.astype(jnp.float32)[None],
        weight,
        bias.astype(jnp.float32)[:, None, :],
        cosines,
        sines,
        cache,
        out_weight,
    )


def per_device(
    hidden_in,
    context_len,
    page_table,
    paged_cache,
    attn_gain,
    proj_weight,
    proj_bias,
    out_weight,
    mlp_gain,
    expert_ids,
    route_weight,
    w_experts_in,
    w_experts_out,
    w_shared_in,
    w_shared_out,
    shared_gate,
):
    tok_rows, width = hidden_in.shape
    half = width // 2
    head_lanes = lax.axis_size("head")
    device_count = lax.axis_size("tok") * head_lanes
    expert_count = device_count // 2
    top_count = expert_ids.shape[1]
    capacity = 2 * max(1, tok_rows * top_count * 5 // (8 * expert_count))
    slots = expert_count * capacity
    core = lax.axis_index("head") % 2
    swap = [(lane, lane ^ 1) for lane in range(head_lanes)]

    named = expert_ids[:, :, None] == jnp.arange(expert_count, dtype=jnp.int32)
    chosen = jnp.any(named, axis=1)
    share = jnp.sum(jnp.where(named, route_weight[:, :, None], 0.0), axis=1)
    row_ids = jnp.arange(tok_rows, dtype=jnp.int32)
    below = (row_ids[:, None] > row_ids[None, :]).astype(jnp.bfloat16)
    earlier = jnp.dot(below, chosen.astype(jnp.bfloat16), preferred_element_type=jnp.float32)
    spot = jnp.where(chosen, earlier.astype(jnp.int32), -1)
    taken = spot.T[:, None, :] == jnp.arange(capacity, dtype=jnp.int32)[None, :, None]
    dispatch = taken.astype(jnp.bfloat16).reshape(slots, tok_rows)
    combine = jnp.where(taken, share.T[:, None, :], 0.0).reshape(slots, tok_rows)
    combine_high = combine.astype(jnp.bfloat16)
    combine_low = (combine - combine_high.astype(jnp.float32)).astype(jnp.bfloat16)

    gathered = lax.all_gather(hidden_in, "head", axis=0, tiled=True)
    attn_part = attend(
        gathered, context_len, page_table, paged_cache, attn_gain, proj_weight, proj_bias, out_weight
    )
    attn_own = lax.psum_scatter(attn_part, "head", scatter_dimension=0, tiled=True)
    resid = (hidden_in.astype(jnp.float32) + attn_own.astype(jnp.float32)).astype(jnp.bfloat16)
    mixed = rms_scale(resid, mlp_gain)

    buffer = [
        jnp.dot(dispatch, mixed[:, at : at + half], preferred_element_type=jnp.float32)
        .astype(jnp.bfloat16)
        .reshape(expert_count, capacity, half)
        for at in (0, half)
    ]
    sending = jnp.stack(buffer, axis=1).reshape(device_count, capacity, half)
    arrived = lax.all_to_all(sending, ("tok", "head"), split_axis=0, concat_axis=0, tiled=True)

    mixed_all = lax.all_gather(mixed, "head", axis=0, tiled=True)
    inner = jnp.einsum("td,dcf->tcf", mixed_all, w_shared_in, preferred_element_type=jnp.float32)
    activated = (jax.nn.silu(inner[:, 0]) * inner[:, 1]).astype(jnp.bfloat16)
    shared_part = jnp.dot(activated, w_shared_out, preferred_element_type=jnp.float32).astype(
        jnp.bfloat16
    )
    arrived, shared_part = lax.optimization_barrier((arrived, shared_part))
    shared_own = lax.psum_scatter(
        shared_part, "head", scatter_dimension=0, tiled=True
    ).astype(jnp.float32)
    gate = jax.nn.sigmoid(jnp.dot(mixed, shared_gate, preferred_element_type=jnp.float32))

    own = arrived.reshape(device_count * capacity, half)
    other = lax.ppermute(own, "head", swap)
    tokens = jnp.concatenate(
        [jnp.where(core == 0, own, other), jnp.where(core == 0, other, own)], axis=1
    )
    inner = jnp.dot(tokens, w_experts_in[0], preferred_element_type=jnp.float32)
    middle = inner.shape[1] // 2
    activated = (jax.nn.silu(inner[:, :middle]) * inner[:, middle:]).astype(jnp.bfloat16)
    finished = jnp.dot(activated, w_experts_out[0], preferred_element_type=jnp.float32).astype(
        jnp.bfloat16
    )
    low, high = finished[:, :half], finished[:, half:]
    partner = lax.ppermute(jnp.where(core == 0, high, low), "head", swap)
    merged = (
        jnp.where(core == 0, low, high).astype(jnp.float32) + partner.astype(jnp.float32)
    ).astype(jnp.bfloat16)
    returned = lax.all_to_all(
        merged.reshape(device_count, capacity, half),
        ("tok", "head"),
        split_axis=0,
        concat_axis=0,
        tiled=True,
    ).reshape(expert_count, 2, capacity, half)
    routed = []
    for side in range(2):
        part = returned[:, side].reshape(slots, half)
        routed.append(
            lax.dot_general(combine_high, part, DOWN, preferred_element_type=jnp.float32)
            + lax.dot_general(combine_low, part, DOWN, preferred_element_type=jnp.float32)
        )
    routed = jnp.concatenate(routed, axis=1)
    return (resid.astype(jnp.float32) + gate[:, None] * shared_own + routed).astype(jnp.bfloat16)


def solution(mesh):
    in_specs = (
        P(("tok", "head"), None),
        P("tok"),
        P("tok", None),
        P(None, "tok", None, "head"),
        P(),
        P(None, None, "head"),
        P(None, "head"),
        P("head", None),
        P(),
        P(("tok", "head"), None),
        P(("tok", "head"), None),
        P(("tok", "head"), None, None),
        P(("tok", "head"), None, None),
        P(None, None, "head"),
        P("head", None),
        P(),
    )
    out_specs = P(("tok", "head"), None)
    return jax.shard_map(
        per_device, mesh=mesh, in_specs=in_specs, out_specs=out_specs, check_vma=False
    )
```

```python
import math

import jax
import jax.numpy as jnp
from jax import lax
from jax.experimental import pallas as pl
from jax.experimental.pallas import tpu as pltpu
from jax.sharding import PartitionSpec as P

HD = 128
BLOCK = 256
DEEP = (((1,), (1,)), ((), ()))
DOWN = (((0,), (0,)), ((), ()))


EPS = 1e-06
THETA = 1000000.0


def rms_scale(values, gain):
    wide = values.astype(jnp.float32)
    spread = jnp.mean(wide * wide, axis=-1, keepdims=True)
    return (wide * lax.rsqrt(spread + EPS) * gain.astype(jnp.float32)).astype(jnp.bfloat16)


def attend_kernel(
    table, context_len, rows, gain, weight, bias, query_pos, key_pos, cosines, sines, cache, out_weight, out, q_all, k_all, v_all
):
    stretch, width = rows.shape
    lanes = weight.shape[2]
    heads = lanes // HD
    pages, page = cache.shape[1], cache.shape[2]
    span = pages * page
    context = context_len[0]

    @pl.loop(0, pages)
    def _(index):
        place = table[0, index]
        at = pl.ds(pl.multiple_of(index * page, page), page)
        k_all[at, :] = cache[0, place]
        v_all[at, :] = cache[1, place]

    @pl.loop(0, stretch // BLOCK)
    def _(block):
        start = pl.multiple_of(block * BLOCK, BLOCK)
        at = pl.ds(start, BLOCK)
        new_at = pl.ds(pl.multiple_of(span + start, BLOCK), BLOCK)
        wide = rows[at, :].astype(jnp.float32)
        spread = jnp.mean(wide * wide, axis=-1, keepdims=True)
        normed = (wide * lax.rsqrt(spread + EPS) * gain[...]).astype(jnp.bfloat16)
        cos, sin = cosines[at, :], sines[at, :]
        for part, kept, place in ((0, q_all, at), (1, k_all, new_at), (2, v_all, new_at)):
            value = jnp.dot(normed, weight[part], preferred_element_type=jnp.float32) + bias[part]
            if part < 2:
                turned = []
                for head in range(heads):
                    one = value[:, head * HD : (head + 1) * HD]
                    turned.append(one * cos + pltpu.roll(one, HD // 2, 1) * sin)
                value = jnp.concatenate(turned, axis=1)
            kept[place, :] = value.astype(jnp.bfloat16)

    factor = math.log2(math.e) / math.sqrt(HD)

    @pl.loop(0, stretch // BLOCK)
    def _(block):
        start = pl.multiple_of(block * BLOCK, BLOCK)
        at = pl.ds(start, BLOCK)
        old_ok = lax.broadcasted_iota(jnp.int32, (BLOCK, span), 1) < context
        new_ok = key_pos[...] <= query_pos[at, :]
        found = []
        for head in range(heads):
            cols = slice(head * HD, (head + 1) * HD)
            query = q_all[at, cols]
            old = lax.dot_general(query, k_all[:span, cols], DEEP, preferred_element_type=jnp.float32)
            new = lax.dot_general(query, k_all[span:, cols], DEEP, preferred_element_type=jnp.float32)
            old = jnp.where(old_ok, old, -1e30)
            new = jnp.where(new_ok, new, -1e30)
            largest = jnp.maximum(
                jnp.max(old, axis=-1, keepdims=True), jnp.max(new, axis=-1, keepdims=True)
            )
            old = jnp.exp2((old - largest) * factor)
            new = jnp.exp2((new - largest) * factor)
            total = jnp.sum(old, axis=-1, keepdims=True) + jnp.sum(new, axis=-1, keepdims=True)
            value = jnp.dot(
                old.astype(jnp.bfloat16), v_all[:span, cols], preferred_element_type=jnp.float32
            ) + jnp.dot(
                new.astype(jnp.bfloat16), v_all[span:, cols], preferred_element_type=jnp.float32
            )
            found.append((value / total).astype(jnp.bfloat16))
        out[at, :] = jnp.dot(
            jnp.concatenate(found, axis=1), out_weight[...], preferred_element_type=jnp.float32
        ).astype(jnp.bfloat16)


def lane_swap(values, bit, lanes):
    return lax.ppermute(values, "head", [(lane, lane ^ bit) for lane in range(lanes)])


def lane_order(lanes):
    order, bit = [0], lanes // 2
    while bit:
        order, bit = order + [step ^ bit for step in order], bit // 2
    return order


def gather_lanes(values, lanes):
    bit = lanes // 2
    while bit:
        values = jnp.concatenate([values, lane_swap(values, bit, lanes)], axis=0)
        bit //= 2
    return values


def sum_lanes(values, lanes):
    total, bit = values, 1
    while bit < lanes:
        kept = total.shape[0] // 2
        arrived = lane_swap(total[kept:].astype(jnp.bfloat16), bit, lanes)
        total = total[:kept].astype(jnp.float32) + arrived.astype(jnp.float32)
        bit *= 2
    return total


def attend(gathered, order, context_len, page_table, cache, gain, weight, bias, out_weight):
    stretch, width = gathered.shape
    lanes = weight.shape[2]
    span = cache.shape[1] * cache.shape[2]
    frequency = THETA ** (-(jnp.arange(HD // 2, dtype=jnp.float32) * 2.0 / HD))
    positions = context_len[0] + order
    angles = positions.astype(jnp.float32)[:, None] * frequency[None, :]
    cosines = jnp.tile(jnp.cos(angles), (1, 2))
    sines = jnp.sin(angles)
    sines = jnp.concatenate([-sines, sines], axis=1)
    smem = pl.BlockSpec(memory_space=pltpu.SMEM)
    vmem = pl.BlockSpec(memory_space=pltpu.VMEM)
    return pl.pallas_call(
        attend_kernel,
        out_shape=jax.ShapeDtypeStruct((stretch, width), jnp.bfloat16),
        in_specs=[smem, smem] + [vmem] * 10,
        out_specs=vmem,
        scratch_shapes=[
            pltpu.VMEM((stretch, lanes), jnp.bfloat16),
            pltpu.VMEM((span + stretch, lanes), jnp.bfloat16),
            pltpu.VMEM((span + stretch, lanes), jnp.bfloat16),
        ],
        compiler_params=pltpu.CompilerParams(vmem_limit_bytes=52 * 1024 * 1024),
        cost_estimate=pl.CostEstimate(
            flops=12 * 10**9, bytes_accessed=20 * 10**6, transcendentals=5 * 10**6
        ),
    )(
        page_table,
        context_len,
        gathered,
        gain.astype(jnp.float32)[None],
        weight,
        bias.astype(jnp.float32)[:, None, :],
        order[:, None],
        order[None, :],
        cosines,
        sines,
        cache,
        out_weight,
    )


def per_device(
    hidden_in,
    context_len,
    page_table,
    paged_cache,
    attn_gain,
    proj_weight,
    proj_bias,
    out_weight,
    mlp_gain,
    expert_ids,
    route_weight,
    w_experts_in,
    w_experts_out,
    w_shared_in,
    w_shared_out,
    shared_gate,
):
    tok_rows, width = hidden_in.shape
    half = width // 2
    head_lanes = lax.axis_size("head")
    device_count = lax.axis_size("tok") * head_lanes
    expert_count = device_count // 2
    top_count = expert_ids.shape[1]
    capacity = 2 * max(1, tok_rows * top_count * 5 // (8 * expert_count))
    slots = expert_count * capacity
    core = lax.axis_index("head") % 2
    swap = [(lane, lane ^ 1) for lane in range(head_lanes)]

    named = expert_ids[:, :, None] == jnp.arange(expert_count, dtype=jnp.int32)
    chosen = jnp.any(named, axis=1)
    share = jnp.sum(jnp.where(named, route_weight[:, :, None], 0.0), axis=1)
    row_ids = jnp.arange(tok_rows, dtype=jnp.int32)
    below = (row_ids[:, None] > row_ids[None, :]).astype(jnp.bfloat16)
    earlier = jnp.dot(below, chosen.astype(jnp.bfloat16), preferred_element_type=jnp.float32)
    spot = jnp.where(chosen, earlier.astype(jnp.int32), -1)
    taken = spot.T[:, None, :] == jnp.arange(capacity, dtype=jnp.int32)[None, :, None]
    dispatch = taken.astype(jnp.bfloat16).reshape(slots, tok_rows)
    combine = jnp.where(taken, share.T[:, None, :], 0.0).reshape(slots, tok_rows)
    combine_high = combine.astype(jnp.bfloat16)
    combine_low = (combine - combine_high.astype(jnp.float32)).astype(jnp.bfloat16)

    gathered = gather_lanes(hidden_in, head_lanes)
    owners = jnp.array(lane_order(head_lanes), jnp.int32) ^ lax.axis_index("head")
    order = (owners[:, None] * tok_rows + row_ids[None, :]).reshape(-1)
    attn_part = attend(
        gathered, order, context_len, page_table, paged_cache, attn_gain, proj_weight, proj_bias, out_weight
    )
    attn_own = sum_lanes(attn_part, head_lanes)
    resid = (hidden_in.astype(jnp.float32) + attn_own).astype(jnp.bfloat16)
    mixed = rms_scale(resid, mlp_gain)

    buffer = [
        jnp.dot(dispatch, mixed[:, at : at + half], preferred_element_type=jnp.float32)
        .astype(jnp.bfloat16)
        .reshape(expert_count, capacity, half)
        for at in (0, half)
    ]
    sending = jnp.stack(buffer, axis=1).reshape(device_count, capacity, half)
    arrived = lax.all_to_all(sending, ("tok", "head"), split_axis=0, concat_axis=0, tiled=True)

    mixed_all = gather_lanes(mixed, head_lanes)
    inner = jnp.einsum("td,dcf->tcf", mixed_all, w_shared_in, preferred_element_type=jnp.float32)
    activated = (jax.nn.silu(inner[:, 0]) * inner[:, 1]).astype(jnp.bfloat16)
    shared_part = jnp.dot(activated, w_shared_out, preferred_element_type=jnp.float32).astype(
        jnp.bfloat16
    )
    arrived, shared_part = lax.optimization_barrier((arrived, shared_part))
    shared_own = sum_lanes(shared_part, head_lanes)
    gate = jax.nn.sigmoid(jnp.dot(mixed, shared_gate, preferred_element_type=jnp.float32))

    own = arrived.reshape(device_count * capacity, half)
    other = lax.ppermute(own, "head", swap)
    tokens = jnp.concatenate(
        [jnp.where(core == 0, own, other), jnp.where(core == 0, other, own)], axis=1
    )
    inner = jnp.dot(tokens, w_experts_in[0], preferred_element_type=jnp.float32)
    middle = inner.shape[1] // 2
    activated = (jax.nn.silu(inner[:, :middle]) * inner[:, middle:]).astype(jnp.bfloat16)
    finished = jnp.dot(activated, w_experts_out[0], preferred_element_type=jnp.float32).astype(
        jnp.bfloat16
    )
    low, high = finished[:, :half], finished[:, half:]
    partner = lax.ppermute(jnp.where(core == 0, high, low), "head", swap)
    merged = (
        jnp.where(core == 0, low, high).astype(jnp.float32) + partner.astype(jnp.float32)
    ).astype(jnp.bfloat16)
    returned = lax.all_to_all(
        merged.reshape(device_count, capacity, half),
        ("tok", "head"),
        split_axis=0,
        concat_axis=0,
        tiled=True,
    ).reshape(expert_count, 2, capacity, half)
    routed = []
    for side in range(2):
        part = returned[:, side].reshape(slots, half)
        routed.append(
            lax.dot_general(combine_high, part, DOWN, preferred_element_type=jnp.float32)
            + lax.dot_general(combine_low, part, DOWN, preferred_element_type=jnp.float32)
        )
    routed = jnp.concatenate(routed, axis=1)
    return (resid.astype(jnp.float32) + gate[:, None] * shared_own + routed).astype(jnp.bfloat16)


def solution(mesh):
    in_specs = (
        P(("tok", "head"), None),
        P("tok"),
        P("tok", None),
        P(None, "tok", None, "head"),
        P(),
        P(None, None, "head"),
        P(None, "head"),
        P("head", None),
        P(),
        P(("tok", "head"), None),
        P(("tok", "head"), None),
        P(("tok", "head"), None, None),
        P(("tok", "head"), None, None),
        P(None, None, "head"),
        P("head", None),
        P(),
    )
    out_specs = P(("tok", "head"), None)
    return jax.shard_map(
        per_device, mesh=mesh, in_specs=in_specs, out_specs=out_specs, check_vma=False
    )
```

```python
import math

import jax
import jax.numpy as jnp
from jax import lax
from jax.experimental import pallas as pl
from jax.experimental.pallas import tpu as pltpu
from jax.sharding import PartitionSpec as P

HD = 128
BLOCK = 256
DEEP = (((1,), (1,)), ((), ()))
DOWN = (((0,), (0,)), ((), ()))


EPS = 1e-06
THETA = 1000000.0


def rms_scale(values, gain):
    wide = values.astype(jnp.float32)
    spread = jnp.mean(wide * wide, axis=-1, keepdims=True)
    return (wide * lax.rsqrt(spread + EPS) * gain.astype(jnp.float32)).astype(jnp.bfloat16)


def attend_kernel(
    table, context_len, rows, gain, weight, bias, query_pos, key_pos, cosines, sines, cache, out_weight, out, q_all, k_all, v_all
):
    stretch, width = rows.shape
    lanes = weight.shape[2]
    heads = lanes // HD
    pages, page = cache.shape[1], cache.shape[2]
    span = pages * page
    context = context_len[0]

    @pl.loop(0, pages)
    def _(index):
        place = table[0, index]
        at = pl.ds(pl.multiple_of(index * page, page), page)
        k_all[at, :] = cache[0, place]
        v_all[at, :] = cache[1, place]

    @pl.loop(0, stretch // BLOCK)
    def _(block):
        start = pl.multiple_of(block * BLOCK, BLOCK)
        at = pl.ds(start, BLOCK)
        new_at = pl.ds(pl.multiple_of(span + start, BLOCK), BLOCK)
        wide = rows[at, :].astype(jnp.float32)
        spread = jnp.mean(wide * wide, axis=-1, keepdims=True)
        normed = (wide * lax.rsqrt(spread + EPS) * gain[...]).astype(jnp.bfloat16)
        cos, sin = cosines[at, :], sines[at, :]
        for part, kept, place in ((0, q_all, at), (1, k_all, new_at), (2, v_all, new_at)):
            value = jnp.dot(normed, weight[part], preferred_element_type=jnp.float32) + bias[part]
            if part < 2:
                turned = []
                for head in range(heads):
                    one = value[:, head * HD : (head + 1) * HD]
                    turned.append(one * cos + pltpu.roll(one, HD // 2, 1) * sin)
                value = jnp.concatenate(turned, axis=1)
            kept[place, :] = value.astype(jnp.bfloat16)

    factor = math.log2(math.e) / math.sqrt(HD)

    @pl.loop(0, stretch // BLOCK)
    def _(block):
        start = pl.multiple_of(block * BLOCK, BLOCK)
        at = pl.ds(start, BLOCK)
        old_ok = lax.broadcasted_iota(jnp.int32, (BLOCK, span), 1) < context
        new_ok = key_pos[...] <= query_pos[at, :]
        found = []
        for head in range(heads):
            cols = slice(head * HD, (head + 1) * HD)
            query = q_all[at, cols]
            old = lax.dot_general(query, k_all[:span, cols], DEEP, preferred_element_type=jnp.float32)
            new = lax.dot_general(query, k_all[span:, cols], DEEP, preferred_element_type=jnp.float32)
            old = jnp.where(old_ok, old, -1e30)
            new = jnp.where(new_ok, new, -1e30)
            largest = jnp.maximum(
                jnp.max(old, axis=-1, keepdims=True), jnp.max(new, axis=-1, keepdims=True)
            )
            old = jnp.exp2((old - largest) * factor)
            new = jnp.exp2((new - largest) * factor)
            total = jnp.sum(old, axis=-1, keepdims=True) + jnp.sum(new, axis=-1, keepdims=True)
            value = jnp.dot(
                old.astype(jnp.bfloat16), v_all[:span, cols], preferred_element_type=jnp.float32
            ) + jnp.dot(
                new.astype(jnp.bfloat16), v_all[span:, cols], preferred_element_type=jnp.float32
            )
            found.append((value / total).astype(jnp.bfloat16))
        out[at, :] = jnp.dot(
            jnp.concatenate(found, axis=1), out_weight[...], preferred_element_type=jnp.float32
        ).astype(jnp.bfloat16)


def lane_swap(values, bit, lanes):
    return lax.ppermute(values, "head", [(lane, lane ^ bit) for lane in range(lanes)])


def lane_order(lanes):
    order, bit = [0], lanes // 2
    while bit:
        order, bit = order + [step ^ bit for step in order], bit // 2
    return order


def gather_lanes(values, lanes, beside=()):
    bit = lanes // 2
    while bit:
        arrived = lane_swap(values, bit, lanes)
        if beside:
            arrived, *beside = lax.optimization_barrier((arrived, *beside))
        values = jnp.concatenate([values, arrived], axis=0)
        bit //= 2
    return (values, *beside)


def sum_lanes(values, lanes):
    total, bit = values, 1
    while bit < lanes:
        kept = total.shape[0] // 2
        arrived = lane_swap(total[kept:].astype(jnp.bfloat16), bit, lanes)
        total = total[:kept].astype(jnp.float32) + arrived.astype(jnp.float32)
        bit *= 2
    return total


def turn_tables(order, context_len):
    frequency = THETA ** (-(jnp.arange(HD // 2, dtype=jnp.float32) * 2.0 / HD))
    positions = context_len[0] + order
    angles = positions.astype(jnp.float32)[:, None] * frequency[None, :]
    cosines = jnp.tile(jnp.cos(angles), (1, 2))
    sines = jnp.sin(angles)
    sines = jnp.concatenate([-sines, sines], axis=1)
    return cosines, sines


def attend(gathered, order, cosines, sines, context_len, page_table, cache, gain, weight, bias, out_weight):
    stretch, width = gathered.shape
    lanes = weight.shape[2]
    span = cache.shape[1] * cache.shape[2]
    smem = pl.BlockSpec(memory_space=pltpu.SMEM)
    vmem = pl.BlockSpec(memory_space=pltpu.VMEM)
    return pl.pallas_call(
        attend_kernel,
        out_shape=jax.ShapeDtypeStruct((stretch, width), jnp.bfloat16),
        in_specs=[smem, smem] + [vmem] * 10,
        out_specs=vmem,
        scratch_shapes=[
            pltpu.VMEM((stretch, lanes), jnp.bfloat16),
            pltpu.VMEM((span + stretch, lanes), jnp.bfloat16),
            pltpu.VMEM((span + stretch, lanes), jnp.bfloat16),
        ],
        compiler_params=pltpu.CompilerParams(vmem_limit_bytes=52 * 1024 * 1024),
        cost_estimate=pl.CostEstimate(
            flops=12 * 10**9, bytes_accessed=20 * 10**6, transcendentals=5 * 10**6
        ),
    )(
        page_table,
        context_len,
        gathered,
        gain.astype(jnp.float32)[None],
        weight,
        bias.astype(jnp.float32)[:, None, :],
        order[:, None],
        order[None, :],
        cosines,
        sines,
        cache,
        out_weight,
    )


def per_device(
    hidden_in,
    context_len,
    page_table,
    paged_cache,
    attn_gain,
    proj_weight,
    proj_bias,
    out_weight,
    mlp_gain,
    expert_ids,
    route_weight,
    w_experts_in,
    w_experts_out,
    w_shared_in,
    w_shared_out,
    shared_gate,
):
    tok_rows, width = hidden_in.shape
    half = width // 2
    head_lanes = lax.axis_size("head")
    device_count = lax.axis_size("tok") * head_lanes
    expert_count = device_count // 2
    top_count = expert_ids.shape[1]
    capacity = 2 * max(1, tok_rows * top_count * 5 // (8 * expert_count))
    slots = expert_count * capacity
    core = lax.axis_index("head") % 2
    swap = [(lane, lane ^ 1) for lane in range(head_lanes)]

    named = expert_ids[:, :, None] == jnp.arange(expert_count, dtype=jnp.int32)
    chosen = jnp.any(named, axis=1)
    share = jnp.sum(jnp.where(named, route_weight[:, :, None], 0.0), axis=1)
    row_ids = jnp.arange(tok_rows, dtype=jnp.int32)
    below = (row_ids[:, None] > row_ids[None, :]).astype(jnp.bfloat16)
    earlier = jnp.dot(below, chosen.astype(jnp.bfloat16), preferred_element_type=jnp.float32)
    spot = jnp.where(chosen, earlier.astype(jnp.int32), -1)
    taken = spot.T[:, None, :] == jnp.arange(capacity, dtype=jnp.int32)[None, :, None]
    dispatch = taken.astype(jnp.bfloat16).reshape(slots, tok_rows)
    combine = jnp.where(taken, share.T[:, None, :], 0.0).reshape(slots, tok_rows)
    combine_high = combine.astype(jnp.bfloat16)
    combine_low = (combine - combine_high.astype(jnp.float32)).astype(jnp.bfloat16)

    owners = jnp.array(lane_order(head_lanes), jnp.int32) ^ lax.axis_index("head")
    order = (owners[:, None] * tok_rows + row_ids[None, :]).reshape(-1)
    gathered, cosines, sines = gather_lanes(
        hidden_in, head_lanes, turn_tables(order, context_len)
    )
    attn_part = attend(
        gathered, order, cosines, sines, context_len, page_table, paged_cache, attn_gain, proj_weight, proj_bias, out_weight
    )
    attn_own = sum_lanes(attn_part, head_lanes)
    resid = (hidden_in.astype(jnp.float32) + attn_own).astype(jnp.bfloat16)
    mixed = rms_scale(resid, mlp_gain)

    buffer = [
        jnp.dot(dispatch, mixed[:, at : at + half], preferred_element_type=jnp.float32)
        .astype(jnp.bfloat16)
        .reshape(expert_count, capacity, half)
        for at in (0, half)
    ]
    sending = jnp.stack(buffer, axis=1).reshape(device_count, capacity, half)
    arrived = lax.all_to_all(sending, ("tok", "head"), split_axis=0, concat_axis=0, tiled=True)

    mixed_all = gather_lanes(mixed, head_lanes)[0]
    inner = jnp.einsum("td,dcf->tcf", mixed_all, w_shared_in, preferred_element_type=jnp.float32)
    activated = (jax.nn.silu(inner[:, 0]) * inner[:, 1]).astype(jnp.bfloat16)
    shared_part = jnp.dot(activated, w_shared_out, preferred_element_type=jnp.float32).astype(
        jnp.bfloat16
    )
    arrived, shared_part = lax.optimization_barrier((arrived, shared_part))
    shared_own = sum_lanes(shared_part, head_lanes)
    gate = jax.nn.sigmoid(jnp.dot(mixed, shared_gate, preferred_element_type=jnp.float32))

    own = arrived.reshape(device_count * capacity, half)
    other = lax.ppermute(own, "head", swap)
    tokens = jnp.concatenate(
        [jnp.where(core == 0, own, other), jnp.where(core == 0, other, own)], axis=1
    )
    inner = jnp.dot(tokens, w_experts_in[0], preferred_element_type=jnp.float32)
    middle = inner.shape[1] // 2
    activated = (jax.nn.silu(inner[:, :middle]) * inner[:, middle:]).astype(jnp.bfloat16)
    finished = jnp.dot(activated, w_experts_out[0], preferred_element_type=jnp.float32).astype(
        jnp.bfloat16
    )
    low, high = finished[:, :half], finished[:, half:]
    partner = lax.ppermute(jnp.where(core == 0, high, low), "head", swap)
    merged = (
        jnp.where(core == 0, low, high).astype(jnp.float32) + partner.astype(jnp.float32)
    ).astype(jnp.bfloat16)
    returned = lax.all_to_all(
        merged.reshape(device_count, capacity, half),
        ("tok", "head"),
        split_axis=0,
        concat_axis=0,
        tiled=True,
    ).reshape(expert_count, 2, capacity, half)
    routed = []
    for side in range(2):
        part = returned[:, side].reshape(slots, half)
        routed.append(
            lax.dot_general(combine_high, part, DOWN, preferred_element_type=jnp.float32)
            + lax.dot_general(combine_low, part, DOWN, preferred_element_type=jnp.float32)
        )
    routed = jnp.concatenate(routed, axis=1)
    return (resid.astype(jnp.float32) + gate[:, None] * shared_own + routed).astype(jnp.bfloat16)


def solution(mesh):
    in_specs = (
        P(("tok", "head"), None),
        P("tok"),
        P("tok", None),
        P(None, "tok", None, "head"),
        P(),
        P(None, None, "head"),
        P(None, "head"),
        P("head", None),
        P(),
        P(("tok", "head"), None),
        P(("tok", "head"), None),
        P(("tok", "head"), None, None),
        P(("tok", "head"), None, None),
        P(None, None, "head"),
        P("head", None),
        P(),
    )
    out_specs = P(("tok", "head"), None)
    return jax.shard_map(
        per_device, mesh=mesh, in_specs=in_specs, out_specs=out_specs, check_vma=False
    )
```
